32 devices in a mesh: az: 16 (over z, y, core), dr: 2 (over x).
Axes of the slice: x: 2, y: 2, z: 4, core: 2. Of those that a mesh axis runs over, the one named last changes fastest.
Arguments:
- stack: bfloat16 [2, 32, 384, 4096], P(None, 'dr', 'az'), may hold values from -6 to 6
- range_filter: float32 [32, 4096], P('dr'), may hold values from 0.2 to 1.5
- scatter_mask: int32 [384, 4096], P('az'), may hold values 0 or 1
Outputs:
- phase_vector: float32 [2, 32, 96, 1024], P(None, None, 'az', 'dr')
The draws below stay inside these ranges and needn't reach their ends.
All inputs are finite; a program needn't handle non-finite values. No bound on the sum of `scatter_mask` on one device may be relied on, other than what follows from the above.
Results may differ from the reference program's by a relative error of at most 0.0037.
Values may be sent and summed in bfloat16 or wider, within the bound.
A program may use at most 256 MiB of HBM per device.

```python
import jax
import jax.numpy as jnp
from jax import lax

DATES = 32
RG = 4096
ITERS = 4
AZ = 384


def set_ends(drawn, rng, smallest, top_value):
    longest = drawn.shape.index(max(drawn.shape))
    spots = []
    for shift in (0, 1):
        where = [jax.random.randint(jax.random.fold_in(rng, axis), (), 0, length) for axis, length in enumerate(drawn.shape)]
        where[longest] = (where[longest] + shift) % drawn.shape[longest]
        spots.append(tuple(where))
    return drawn.at[spots[0]].set(smallest).at[spots[1]].set(top_value)


def level_of(own_key, dims, pieces, least, top_value):
    level, own = 1.0, jax.random.fold_in(own_key, 6)
    for dim, shards_of in pieces:
        draws = jnp.exp(jax.random.uniform(jax.random.fold_in(own, dim), (shards_of,), jnp.float32, least / len(pieces), top_value / len(pieces)))
        level = level * jnp.repeat(draws, dims[dim] // shards_of).reshape([-1 if axis == dim else 1 for axis in range(len(dims))])
    return level


def centred(own_key, extent, deviation, limit, cuts=(), held_as=jnp.bfloat16):
    array = jax.random.normal(own_key, extent, jnp.float32) * deviation
    if len(cuts) > 0:
        array = level_of(own_key, extent, cuts, -0.22, 0.18) * array
    return jnp.clip(array, min=-limit, max=limit).astype(held_as)


def setup_inputs(seed: int = 0) -> dict:
    key_list = jax.random.split(jax.random.key(seed), 4)
    return {
        "stack": centred(key_list[0], (2, DATES, AZ, RG), 1.0, 6.0, ((1, 2), (2, 16))),
        "range_filter": jnp.clip(0.2 + 1.3 * jax.random.uniform(key_list[1], (DATES, RG), jnp.float32) ** level_of(key_list[1], (DATES, RG), ((0, 2),), -0.2, 0.2), 0.2, 1.5),
        "scatter_mask": set_ends((jax.random.randint(key_list[2], (AZ, RG), 0, 4) < 3).astype(jnp.int32), jax.random.fold_in(key_list[2], 1), 0, 1),
    }


BETA_LOAD = 1.0
PROJ_LOAD = 1.0

def link_phases(cov_real, cov_imag):
    diagonal = jnp.moveaxis(jnp.diagonal(cov_real, axis1=0, axis2=1), -1, 0)
    scales = jnp.sqrt(diagonal + BETA_LOAD)
    product = scales[:, None] * scales[None, :]
    coh_real = cov_real / product
    coh_imag = cov_imag / product
    vec_real = jnp.ones(diagonal.shape, jnp.float32)
    vec_imag = jnp.zeros(diagonal.shape, jnp.float32)
    for repeat in range(ITERS):
        new_real = lax.optimization_barrier(jnp.sum(coh_real * vec_real[None] - coh_imag * vec_imag[None], axis=1))
        new_imag = lax.optimization_barrier(jnp.sum(coh_real * vec_imag[None] + coh_imag * vec_real[None], axis=1))
        length = jnp.sqrt(new_real * new_real + new_imag * new_imag + PROJ_LOAD)
        vec_real = new_real / length
        vec_imag = new_imag / length
    return jnp.stack([vec_real, vec_imag])

def reference(stack, range_filter, scatter_mask):

    def filter_date(position):
        date_stack = lax.dynamic_index_in_dim(stack, position, 1, keepdims=False)
        gains = lax.dynamic_index_in_dim(range_filter, position, 0, keepdims=False)
        field = date_stack[0].astype(jnp.float32) + 1j * date_stack[1].astype(jnp.float32)
        spectrum = jnp.fft.fft(field, axis=-1) * gains[None, :]
        result = jnp.fft.ifft(spectrum, axis=-1)
        return jnp.stack([jnp.real(result).astype(jnp.bfloat16), jnp.imag(result).astype(jnp.bfloat16)])
    filtered = lax.map(filter_date, jnp.arange(DATES, dtype=jnp.int32))
    filtered = jnp.moveaxis(filtered, 0, 1).reshape(2 * DATES, AZ, RG)
    padded = jnp.pad(filtered, ((0, 0), (6, 6), (6, 6)))
    weight = jnp.pad(scatter_mask, 6).astype(jnp.bfloat16)
    masked = padded * weight[None]
    block_cols = RG // 4 + 3
    windows = RG // 4

    def advance(previous, row_index):
        start = row_index * 4
        plain_rows = lax.dynamic_slice_in_dim(padded, start, 4, 1).astype(jnp.float32).reshape(2 * DATES, 4, block_cols, 4)
        masked_rows = lax.dynamic_slice_in_dim(masked, start, 4, 1).astype(jnp.float32).reshape(2 * DATES, 4, block_cols, 4)
        gram_matrix = jnp.einsum('ajbk,cjbk->acb', masked_rows, plain_rows, precision=lax.Precision.HIGHEST)
        current = jnp.stack([gram_matrix[:DATES, :DATES] + gram_matrix[DATES:, DATES:], gram_matrix[DATES:, :DATES] - gram_matrix[:DATES, DATES:]])
        row_sum = previous[0] + previous[1] + previous[2] + current
        window_sum = row_sum[..., 0:windows] + row_sum[..., 1:windows + 1] + row_sum[..., 2:windows + 2] + row_sum[..., 3:windows + 3]
        phases = link_phases(window_sum[0], window_sum[1])
        return (jnp.concatenate([previous[1:], current[None]], axis=0), phases)
    initial = jnp.zeros((3, 2, DATES, DATES, block_cols), jnp.float32)
    unused, outputs = lax.scan(advance, initial, jnp.arange(AZ // 4 + 3, dtype=jnp.int32))
    return jnp.transpose(outputs[3:], (1, 2, 0, 3))
```

```python
import functools
import math

import jax
import jax.numpy as jnp
import numpy as np
from jax import lax
from jax.experimental import pallas as pl
from jax.experimental.pallas import tpu as pltpu
from jax.sharding import PartitionSpec as P

ITERS = 4
BETA_LOAD = 1.0
PROJ_LOAD = 1.0
LANES = 128
STEP = 256
HALO = 6


def times_const(value, c, s):
    re, im = value
    if abs(s) < 1e-12:
        return (re, im) if c > 0 else (-re, -im)
    if abs(c) < 1e-12:
        return (-im, re) if s > 0 else (im, -re)
    if abs(abs(c) - abs(s)) < 1e-12:
        h = abs(c)
        sc, ss = (1.0 if c > 0 else -1.0), (1.0 if s > 0 else -1.0)
        a = re if sc == 1.0 else -re
        b = im if sc == 1.0 else -im
        return (h * (a - im if ss == 1.0 else a + im), h * (b + re if ss == 1.0 else b - re))
    return (re * c - im * s, re * s + im * c)


def vector_fft(values, sign):
    count = len(values)
    if count == 1:
        return values
    even = vector_fft(values[0::2], sign)
    odd = vector_fft(values[1::2], sign)
    out = [None] * count
    for k in range(count // 2):
        angle = sign * 2.0 * math.pi * k / count
        tr, ti = times_const(odd[k], math.cos(angle), math.sin(angle))
        er, ei = even[k]
        out[k] = (er + tr, ei + ti)
        out[k + count // 2] = (er - tr, ei - ti)
    return out


def filter_kernel(outer, x_ref, gain_ref, twr_ref, twi_ref, fh_ref, fl_ref, bh_ref, bl_ref, out_ref, field, work):
    lines = x_ref.shape[2]
    samples = outer * LANES
    field[...] = x_ref[:, 0].astype(jnp.float32)
    groups = lines // 8

    def forward(g, carry):
        rows = pl.ds(pl.multiple_of(g * 8, 8), 8)
        vals = [
            (field[0, rows, o * LANES : (o + 1) * LANES], field[1, rows, o * LANES : (o + 1) * LANES])
            for o in range(outer)
        ]
        vals = vector_fft(vals, -1.0)
        for o in range(outer):
            re, im = vals[o]
            c, s = twr_ref[o : o + 1, :], twi_ref[o : o + 1, :]
            work[o, rows, 0:LANES] = re * c - im * s
            work[o, rows, LANES:STEP] = re * s + im * c
        return carry

    lax.fori_loop(0, groups, forward, 0)

    def apply(values, high_ref, low_ref):
        high = values.astype(jnp.bfloat16)
        low = (values - high.astype(jnp.float32)).astype(jnp.bfloat16)
        dot = functools.partial(jnp.dot, preferred_element_type=jnp.float32)
        return dot(high, high_ref[...]) + (dot(low, high_ref[...]) + dot(high, low_ref[...]))

    part = 8

    def middle(q, carry):
        span = pl.ds(q * part, part)
        values = work[span].reshape(part * lines, STEP)
        spec = apply(values, fh_ref, fl_ref).reshape(part, lines, STEP)
        gains = gain_ref[0, pl.ds(pl.multiple_of(q * part, part), part), :]
        both = jnp.concatenate([gains, gains], axis=1)[:, None, :]
        spec = (spec * both).reshape(part * lines, STEP)
        work[span] = apply(spec, bh_ref, bl_ref).reshape(part, lines, STEP)
        return carry

    lax.fori_loop(0, outer // part, middle, 0)

    def backward(g, carry):
        rows = pl.ds(pl.multiple_of(g * 8, 8), 8)
        vals = []
        for o in range(outer):
            re, im = work[o, rows, 0:LANES], work[o, rows, LANES:STEP]
            c, s = twr_ref[o : o + 1, :], twi_ref[o : o + 1, :]
            vals.append((re * c + im * s, im * c - re * s))
        vals = vector_fft(vals, 1.0)
        for o in range(outer):
            field[0, rows, o * LANES : (o + 1) * LANES] = vals[o][0] * (1.0 / samples)
            field[1, rows, o * LANES : (o + 1) * LANES] = vals[o][1] * (1.0 / samples)
        return carry

    lax.fori_loop(0, groups, backward, 0)
    out_ref[:, 0] = field[...].astype(jnp.bfloat16)


def split_table(table):
    high = table.astype(jnp.bfloat16)
    return high, (table - np.asarray(high).astype(np.float32)).astype(jnp.bfloat16)


def filter_lines(stack, gains):
    dates, lines, samples = stack.shape[1:]
    outer = samples // LANES
    n = np.arange(LANES)
    angle = -2.0 * np.pi * (n[:, None] * n[None, :] % LANES) / LANES
    c, s = np.cos(angle), np.sin(angle)
    fwd = np.block([[c, s], [-s, c]]).astype(np.float32)
    bwd = np.block([[c, -s], [s, c]]).astype(np.float32)
    twist = -2.0 * np.pi * (np.arange(outer)[:, None] * n[None, :]) / samples
    fh, fl = split_table(fwd)
    bh, bl = split_table(bwd)
    gain_table = jnp.transpose(gains.reshape(dates, LANES, outer), (0, 2, 1))
    whole = lambda *shape: pl.BlockSpec(shape, lambda d: (0,) * len(shape))
    return pl.pallas_call(
        functools.partial(filter_kernel, outer),
        grid=(dates,),
        in_specs=[
            pl.BlockSpec((2, 1, lines, samples), lambda d: (0, d, 0, 0)),
            pl.BlockSpec((1, outer, LANES), lambda d: (d, 0, 0)),
            whole(outer, LANES),
            whole(outer, LANES),
            whole(STEP, STEP),
            whole(STEP, STEP),
            whole(STEP, STEP),
            whole(STEP, STEP),
        ],
        out_specs=pl.BlockSpec((2, 1, lines, samples), lambda d: (0, d, 0, 0)),
        out_shape=jax.ShapeDtypeStruct(stack.shape, jnp.bfloat16),
        scratch_shapes=[
            pltpu.VMEM((2, lines, samples), jnp.float32),
            pltpu.VMEM((outer, lines, STEP), jnp.float32),
        ],
        compiler_params=pltpu.CompilerParams(vmem_limit_bytes=40 * 2**20),
    )(
        stack,
        gain_table,
        np.cos(twist).astype(np.float32),
        np.sin(twist).astype(np.float32),
        fh,
        fl,
        bh,
        bl,
    )


def link_kernel(dates, z_ref, m_ref, band_ref, out_ref, flat, pr, pi, mr, mi, wide, cov_a, cov_b, y_ref, low_ref, diag, m_half):
    step = pl.program_id(0)
    lines = z_ref.shape[1]
    blocks = lines // 4
    wins = blocks - 3
    half = dates // 2
    pitch = flat.shape[1] // (2 * dates)
    rest = wins * 2 * dates

    for p in range(2 * dates):
        rows = z_ref[p].astype(jnp.float32)
        for h in range(2):
            flat[h, p * pitch : p * pitch + lines, :] = rows[:, h * LANES : (h + 1) * LANES]

    for h in range(2):
        m_half[h] = m_ref[:, h * LANES : (h + 1) * LANES]

    def spread(line, carry):
        for h in range(2):
            weight = m_half[h, pl.ds(line, 1), :]
            re = flat[h, pl.ds(line, dates, stride=pitch), :]
            im = flat[h, pl.ds(line + dates * pitch, dates, stride=pitch), :]
            pr[h, line] = re
            pi[h, line] = im
            mr[h, line] = re * weight
            mi[h, line] = im * weight
        return carry

    lax.fori_loop(0, lines, spread, 0)
    odd = step % 2 == 1

    def sums(date, first):
        for h in range(2):
            lanes = slice(h * LANES, (h + 1) * LANES)
            last = None
            pairs = []
            for r in range(blocks):
                re = im = None
                for j in range(4):
                    line = 4 * r + j
                    ar = mr[h, line, pl.ds(date, 1), :]
                    ai = mi[h, line, pl.ds(date, 1), :]
                    br = pr[h, line, first:dates, :]
                    bi = pi[h, line, first:dates, :]
                    t_re = ar * br + ai * bi
                    t_im = ai * br - ar * bi
                    re = t_re if re is None else re + t_re
                    im = t_im if im is None else im + t_im
                if last is not None:
                    pairs.append((last[0] + re, last[1] + im))
                last = (re, im)
                a = r - 3
                if a >= 0:
                    wide[date % 2, a, 0, first:dates, lanes] = (pairs[a][0] + pairs[a + 2][0]).astype(jnp.bfloat16)
                    wide[date % 2, a, 1, first:dates, lanes] = (pairs[a][1] + pairs[a + 2][1]).astype(jnp.bfloat16)

    def gather(date, first):
        rows = wide[date % 2, :, :, first:dates, :].reshape(wins * 2 * (dates - first), STEP)
        total = jnp.dot(rows, band_ref[0], preferred_element_type=jnp.float32)
        total = total.reshape(wins, 2, dates - first, 2 * LANES)
        old = cov_b[date, :, :, first:dates, :]
        cov_a[date, :, :, first:dates, :] = old + total[..., 0:LANES]
        cov_b[date, :, :, first:dates, :] = jnp.where(odd, old, 0.0) + total[..., LANES : 2 * LANES]

    for first, start, stop in ((0, 0, half), (half, half, dates)):
        sums(start, first)

        def body(date, carry, first=first):
            gather(date - 1, first)
            sums(date, first)
            return carry

        lax.fori_loop(start + 1, stop, body, 0)
        gather(stop - 1, first)

    @pl.when((step % 2 == 0) & (step > 0))
    def _():
        def window(a, carry):
            def pick(date, c):
                diag[pl.ds(date, 1), :] = cov_a[date, a, 0, pl.ds(date, 1), :]
                return c

            lax.fori_loop(0, dates, pick, 0)
            inv = 1.0 / jnp.sqrt(diag[...] + BETA_LOAD)
            vec_re = jnp.ones_like(inv)
            vec_im = jnp.zeros_like(inv)
            for repeat in range(ITERS):
                y_ref[0] = vec_re * inv
                y_ref[1] = vec_im * inv
                top_re, top_im = y_ref[0, half:dates], y_ref[1, half:dates]

                def upper(date, acc):
                    acc_re, acc_im = acc
                    c_re, c_im = cov_a[date, a, 0], cov_a[date, a, 1]
                    x_re, x_im = y_ref[0, pl.ds(date, 1), :], y_ref[1, pl.ds(date, 1), :]
                    h_re, h_im = c_re[half:dates], c_im[half:dates]
                    low_ref[0, pl.ds(date, 1), :] = jnp.sum(h_re * top_re - h_im * top_im, axis=0, keepdims=True)
                    low_ref[1, pl.ds(date, 1), :] = jnp.sum(h_re * top_im + h_im * top_re, axis=0, keepdims=True)
                    return (
                        acc_re + (c_re * x_re + c_im * x_im),
                        acc_im + (c_re * x_im - c_im * x_re),
                    )

                def lower(date, acc):
                    acc_re, acc_im = acc
                    c_re, c_im = cov_a[date, a, 0, half:dates], cov_a[date, a, 1, half:dates]
                    x_re, x_im = y_ref[0, pl.ds(date, 1), :], y_ref[1, pl.ds(date, 1), :]
                    return (
                        acc_re + (c_re * x_re + c_im * x_im),
                        acc_im + (c_re * x_im - c_im * x_re),
                    )

                zero = jnp.zeros_like(inv)
                u_re, u_im = lax.fori_loop(0, half, upper, (zero, zero), unroll=4)
                b_re, b_im = lax.fori_loop(half, dates, lower, (u_re[half:], u_im[half:]), unroll=4)
                u_re = jnp.concatenate([u_re[:half] + low_ref[0], b_re], axis=0) * inv
                u_im = jnp.concatenate([u_im[:half] + low_ref[1], b_im], axis=0) * inv
                length = 1.0 / jnp.sqrt(u_re * u_re + u_im * u_im + PROJ_LOAD)
                vec_re = u_re * length
                vec_im = u_im * length
            out_ref[a, 0] = vec_re
            out_ref[a, 1] = vec_im
            return carry

        lax.fori_loop(0, wins, window, 0)


def link_windows(planes, mask, win_cols):
    dates = planes.shape[0] // 2
    lines = planes.shape[1]
    wins = lines // 4 - 3
    chunks = win_cols // LANES
    steps = 2 * chunks + 1
    pitch = -(-lines // 8) * 8
    column = np.arange(STEP)[:, None]
    window = np.arange(LANES)[None, :]
    band = lambda shift: ((column + shift >= 4 * window) & (column + shift < 4 * window + 16)).astype(np.float32)
    zero = np.zeros((STEP, LANES), np.float32)
    bands = np.stack(
        [
            np.concatenate([band(2 * STEP), band(0)], axis=1),
            np.concatenate([zero, band(STEP)], axis=1),
        ]
    ).astype(jnp.bfloat16)
    f32 = jnp.float32
    return pl.pallas_call(
        functools.partial(link_kernel, dates),
        grid=(steps,),
        in_specs=[
            pl.BlockSpec((2 * dates, lines, STEP), lambda t: (0, 0, t)),
            pl.BlockSpec((lines, STEP), lambda t: (0, t)),
            pl.BlockSpec((1, STEP, 2 * LANES), lambda t: (t % 2, 0, 0)),
        ],
        out_specs=pl.BlockSpec((wins, 2, dates, LANES), lambda t: (0, 0, 0, jnp.maximum((t + 1) // 2 - 1, 0))),
        out_shape=jax.ShapeDtypeStruct((wins, 2, dates, win_cols), f32),
        scratch_shapes=[
            pltpu.VMEM((2, 2 * dates * pitch, LANES), f32),
            pltpu.VMEM((2, lines, dates, LANES), f32),
            pltpu.VMEM((2, lines, dates, LANES), f32),
            pltpu.VMEM((2, lines, dates, LANES), f32),
            pltpu.VMEM((2, lines, dates, LANES), f32),
            pltpu.VMEM((2, wins, 2, dates, STEP), jnp.bfloat16),
            pltpu.VMEM((dates, wins, 2, dates, LANES), f32),
            pltpu.VMEM((dates, wins, 2, dates, LANES), f32),
            pltpu.VMEM((2, dates, LANES), f32),
            pltpu.VMEM((2, dates // 2, LANES), f32),
            pltpu.VMEM((dates, LANES), f32),
            pltpu.VMEM((2, lines, LANES), f32),
        ],
        compiler_params=pltpu.CompilerParams(vmem_limit_bytes=56 * 2**20),
    )(planes, mask, bands)


def on_device(stack, range_filter, scatter_mask):
    parts = lax.axis_size("dr")
    own = lax.axis_index("dr")
    dates_here, lines, samples = stack.shape[1:]
    dates = dates_here * parts
    tile = samples // parts
    width = tile + 2 * HALO
    win_cols = tile // 4
    padded_width = STEP * (2 * (win_cols // LANES) + 1)
    filtered = filter_lines(stack, range_filter)
    wide = jnp.pad(filtered, ((0, 0), (0, 0), (0, 0), (HALO, HALO)))

    def cut(array, number):
        return lax.dynamic_slice_in_dim(array, number * tile, width, array.ndim - 1)

    pieces = [cut(wide, own)]
    for shift in range(1, parts):
        sent = cut(wide, lax.rem(own + shift, parts))
        pieces.append(lax.ppermute(sent, "dr", [(i, (i + shift) % parts) for i in range(parts)]))
    planes = jnp.concatenate(pieces, axis=1).reshape(2 * dates, lines, width)
    mask = cut(jnp.pad(scatter_mask, ((0, 0), (HALO, HALO))), own).astype(jnp.bfloat16)

    def halo(array, dim):
        count = lax.axis_size("az")
        head = lax.slice_in_dim(array, 0, HALO, axis=dim)
        tail = lax.slice_in_dim(array, lines - HALO, lines, axis=dim)
        before = lax.ppermute(tail, "az", [(i, i + 1) for i in range(count - 1)])
        after = lax.ppermute(head, "az", [(i + 1, i) for i in range(count - 1)])
        return jnp.concatenate([before, array, after], axis=dim)

    spare = padded_width - width
    planes = jnp.pad(halo(planes, 1), ((0, 0), (0, 0), (0, spare)))
    mask = jnp.pad(halo(mask, 0), ((0, 0), (0, spare))).astype(jnp.float32)
    linked = link_windows(planes, mask, win_cols)
    wins = linked.shape[0]
    linked = jnp.transpose(linked, (1, 2, 0, 3)).reshape(2, parts, dates_here, wins, win_cols)
    ordered = [
        lax.dynamic_index_in_dim(linked, lax.rem(own - t + parts, parts), 1, keepdims=False) for t in range(parts)
    ]
    return jnp.concatenate(ordered, axis=1)


def solution(mesh):
    in_specs = (P(None, "dr", "az", None), P("dr", None), P("az", None))
    out_specs = P(None, None, "az", "dr")
    return jax.shard_map(on_device, mesh=mesh, in_specs=in_specs, out_specs=out_specs, check_vma=False)
```

```python
import functools
import math

import jax
import jax.numpy as jnp
import numpy as np
from jax import lax
from jax.experimental import pallas as pl
from jax.experimental.pallas import tpu as pltpu
from jax.sharding import PartitionSpec as P

ITERS = 4
BETA_LOAD = 1.0
PROJ_LOAD = 1.0
LANES = 128
STEP = 256
HALO = 6
CHUNKS = 2


def times_const(value, c, s):
    re, im = value
    if abs(s) < 1e-12:
        return (re, im) if c > 0 else (-re, -im)
    if abs(c) < 1e-12:
        return (-im, re) if s > 0 else (im, -re)
    if abs(abs(c) - abs(s)) < 1e-12:
        h = abs(c)
        sc, ss = (1.0 if c > 0 else -1.0), (1.0 if s > 0 else -1.0)
        a = re if sc == 1.0 else -re
        b = im if sc == 1.0 else -im
        return (h * (a - im if ss == 1.0 else a + im), h * (b + re if ss == 1.0 else b - re))
    return (re * c - im * s, re * s + im * c)


def vector_fft(values, sign):
    count = len(values)
    if count == 1:
        return values
    even = vector_fft(values[0::2], sign)
    odd = vector_fft(values[1::2], sign)
    out = [None] * count
    for k in range(count // 2):
        angle = sign * 2.0 * math.pi * k / count
        tr, ti = times_const(odd[k], math.cos(angle), math.sin(angle))
        er, ei = even[k]
        out[k] = (er + tr, ei + ti)
        out[k + count // 2] = (er - tr, ei - ti)
    return out


def filter_kernel(outer, x_ref, gain_ref, twr_ref, twi_ref, tab_ref, out_ref, field, work):
    lines = x_ref.shape[2]
    samples = outer * LANES
    field[...] = x_ref[:, 0].astype(jnp.float32)
    groups = lines // 8

    def forward(g, carry):
        rows = pl.ds(pl.multiple_of(g * 8, 8), 8)
        vals = [
            (field[0, rows, o * LANES : (o + 1) * LANES], field[1, rows, o * LANES : (o + 1) * LANES])
            for o in range(outer)
        ]
        vals = vector_fft(vals, -1.0)
        for o in range(outer):
            re, im = vals[o]
            c, s = twr_ref[o : o + 1, :], twi_ref[o : o + 1, :]
            work[o, rows, 0:LANES] = re * c - im * s
            work[o, rows, LANES:STEP] = re * s + im * c
        return carry

    lax.fori_loop(0, groups, forward, 0)

    def apply(values, way):
        high = values.astype(jnp.bfloat16)
        low = (values - high.astype(jnp.float32)).astype(jnp.bfloat16)
        dot = functools.partial(jnp.dot, preferred_element_type=jnp.float32)
        return dot(high, tab_ref[way]) + (dot(low, tab_ref[way]) + dot(high, tab_ref[way + 2]))

    part = 8

    def middle(q, carry):
        span = pl.ds(q * part, part)
        values = work[span].reshape(part * lines, STEP)
        spec = apply(values, 0).reshape(part, lines, STEP)
        gains = gain_ref[0, pl.ds(pl.multiple_of(q * part, part), part), :]
        both = jnp.concatenate([gains, gains], axis=1)[:, None, :]
        spec = (spec * both).reshape(part * lines, STEP)
        work[span] = apply(spec, 1).reshape(part, lines, STEP)
        return carry

    lax.fori_loop(0, outer // part, middle, 0)

    def backward(g, carry):
        rows = pl.ds(pl.multiple_of(g * 8, 8), 8)
        vals = []
        for o in range(outer):
            re, im = work[o, rows, 0:LANES], work[o, rows, LANES:STEP]
            c, s = twr_ref[o : o + 1, :], twi_ref[o : o + 1, :]
            vals.append((re * c + im * s, im * c - re * s))
        vals = vector_fft(vals, 1.0)
        for o in range(outer):
            field[0, rows, o * LANES : (o + 1) * LANES] = vals[o][0] * (1.0 / samples)
            field[1, rows, o * LANES : (o + 1) * LANES] = vals[o][1] * (1.0 / samples)
        return carry

    lax.fori_loop(0, groups, backward, 0)
    out_ref[:, 0] = field[...].astype(jnp.bfloat16)


def split_table(table):
    high = table.astype(jnp.bfloat16)
    return high, (table - np.asarray(high).astype(np.float32)).astype(jnp.bfloat16)


def filter_lines(stack, gains, chunk, chunks):
    dates, lines, samples = stack.shape[1:]
    here = dates // chunks
    skip = chunk * here
    outer = samples // LANES
    n = np.arange(LANES)
    angle = -2.0 * np.pi * (n[:, None] * n[None, :] % LANES) / LANES
    c, s = np.cos(angle), np.sin(angle)
    fwd = np.block([[c, s], [-s, c]]).astype(np.float32)
    bwd = np.block([[c, -s], [s, c]]).astype(np.float32)
    twist = -2.0 * np.pi * (np.arange(outer)[:, None] * n[None, :]) / samples
    fh, fl = split_table(fwd)
    bh, bl = split_table(bwd)
    gain_table = jnp.transpose(gains.reshape(dates, LANES, outer), (0, 2, 1))
    whole = lambda *shape: pl.BlockSpec(shape, lambda d: (0,) * len(shape))
    return pl.pallas_call(
        functools.partial(filter_kernel, outer),
        grid=(here,),
        in_specs=[
            pl.BlockSpec((2, 1, lines, samples), lambda d: (0, d + skip, 0, 0)),
            pl.BlockSpec((1, outer, LANES), lambda d: (d + skip, 0, 0)),
            whole(outer, LANES),
            whole(outer, LANES),
            whole(4, STEP, STEP),
        ],
        out_specs=pl.BlockSpec((2, 1, lines, samples), lambda d: (0, d, 0, 0)),
        out_shape=jax.ShapeDtypeStruct((2, here, lines, samples), jnp.bfloat16),
        cost_estimate=pl.CostEstimate(flops=here * 10**8, bytes_accessed=10**6, transcendentals=0),
        scratch_shapes=[
            pltpu.VMEM((2, lines, samples), jnp.float32),
            pltpu.VMEM((outer, lines, STEP), jnp.float32),
        ],
        compiler_params=pltpu.CompilerParams(vmem_limit_bytes=40 * 2**20),
    )(
        stack,
        gain_table,
        np.cos(twist).astype(np.float32),
        np.sin(twist).astype(np.float32),
        np.stack([fh, bh, fl, bl]),
    )


def load_planes(groups, m_ref, flat, pr, pi, mr, mi, m_half):
    count, lines = groups[0].shape[1:3]
    dates = count * len(groups)
    pitch = flat.shape[1] // (2 * dates)
    for part in range(2):
        for k, ref in enumerate(groups):
            for p in range(count):
                rows = ref[part, p].astype(jnp.float32)
                place = (part * dates + k * count + p) * pitch
                for h in range(2):
                    flat[h, place : place + lines, :] = rows[:, h * LANES : (h + 1) * LANES]
    for h in range(2):
        m_half[h] = m_ref[:, h * LANES : (h + 1) * LANES]

    def spread(line, carry):
        for h in range(2):
            weight = m_half[h, pl.ds(line, 1), :]
            re = flat[h, pl.ds(line, dates, stride=pitch), :]
            im = flat[h, pl.ds(line + dates * pitch, dates, stride=pitch), :]
            pr[h, line] = re[dates - count :]
            pi[h, line] = im[dates - count :]
            mr[h, line] = re * weight
            mi[h, line] = im * weight
        return carry

    lax.fori_loop(0, lines, spread, 0)


def window_sums(dates, odd, band_ref, pr, pi, mr, mi, wide, cov_a, cov_b):
    count = pr.shape[2]
    blocks = pr.shape[1] // 4
    wins = blocks - 3

    def sums(slot, spot, date):
        for h in range(2):
            lanes = slice(h * LANES, (h + 1) * LANES)
            last = None
            pairs = []
            for r in range(blocks):
                re = im = None
                for j in range(4):
                    line = 4 * r + j
                    ar = mr[h, line, pl.ds(date, 1), :]
                    ai = mi[h, line, pl.ds(date, 1), :]
                    br = pr[h, line]
                    bi = pi[h, line]
                    t_re = ar * br + ai * bi
                    t_im = ai * br - ar * bi
                    re = t_re if re is None else re + t_re
                    im = t_im if im is None else im + t_im
                if last is not None:
                    pairs.append((last[0] + re, last[1] + im))
                last = (re, im)
                a = r - 3
                if a >= 0:
                    wide[slot, spot, a, 0, :, lanes] = (pairs[a][0] + pairs[a + 2][0]).astype(jnp.bfloat16)
                    wide[slot, spot, a, 1, :, lanes] = (pairs[a][1] + pairs[a + 2][1]).astype(jnp.bfloat16)

    def gather(duo):
        rows = wide[duo % 2].reshape(2 * wins * 2 * count, STEP)
        total = jnp.dot(rows, band_ref[0], preferred_element_type=jnp.float32)
        total = total.reshape(2, wins, 2, count, 2 * LANES)
        span = pl.ds(2 * duo, 2)
        old = cov_b[span]
        cov_a[span] = old + total[..., 0:LANES]
        cov_b[span] = jnp.where(odd, old, 0.0) + total[..., LANES : 2 * LANES]

    def both(duo):
        for spot in range(2):
            sums(duo % 2, spot, 2 * duo + spot)

    both(0)

    def body(duo, carry):
        gather(duo - 1)
        both(duo)
        return carry

    lax.fori_loop(1, dates // 2, body, 0)
    gather(dates // 2 - 1)


def own_kernel(z_ref, m_ref, band_ref, cov_ref, flat, pr, pi, mr, mi, m_half, wide, cov_b):
    load_planes([z_ref], m_ref, flat, pr, pi, mr, mi, m_half)
    odd = pl.program_id(0) % 2 == 1
    window_sums(z_ref.shape[1], odd, band_ref, pr, pi, mr, mi, wide, cov_ref, cov_b)


def link_kernel(
    z_ref, z2_ref, m_ref, band_ref, own_ref, out_ref, flat, pr, pi, mr, mi, m_half, wide, cov_b, cov_a, y_ref, low_ref, diag
):
    step = pl.program_id(0)
    half, lines = z_ref.shape[1:3]
    dates = 2 * half
    wins = lines // 4 - 3
    load_planes([z_ref, z2_ref], m_ref, flat, pr, pi, mr, mi, m_half)
    window_sums(dates, step % 2 == 1, band_ref, pr, pi, mr, mi, wide, cov_a, cov_b)

    @pl.when((step % 2 == 0) & (step > 0))
    def _():
        def window(a, carry):
            def pick(date, c):
                diag[pl.ds(date, 1), :] = own_ref[date, a, 0, pl.ds(date, 1), :]
                diag[pl.ds(date + half, 1), :] = cov_a[date + half, a, 0, pl.ds(date, 1), :]
                return c

            lax.fori_loop(0, half, pick, 0)
            inv = 1.0 / jnp.sqrt(diag[...] + BETA_LOAD)
            vec_re = jnp.ones_like(inv)
            vec_im = jnp.zeros_like(inv)

            def add(acc, c_re, c_im, x_re, x_im):
                return (acc[0] + (c_re * x_re + c_im * x_im), acc[1] + (c_re * x_im - c_im * x_re))

            for repeat in range(ITERS):
                y_ref[0] = vec_re * inv
                y_ref[1] = vec_im * inv
                far_re, far_im = y_ref[0, half:dates], y_ref[1, half:dates]

                def turn(date, acc):
                    near, far = acc
                    x_re, x_im = y_ref[0, pl.ds(date, 1), :], y_ref[1, pl.ds(date, 1), :]
                    w_re, w_im = y_ref[0, pl.ds(date + half, 1), :], y_ref[1, pl.ds(date + half, 1), :]
                    h_re, h_im = cov_a[date, a, 0], cov_a[date, a, 1]
                    low_ref[0, pl.ds(date, 1), :] = jnp.sum(h_re * far_re - h_im * far_im, axis=0, keepdims=True)
                    low_ref[1, pl.ds(date, 1), :] = jnp.sum(h_re * far_im + h_im * far_re, axis=0, keepdims=True)
                    near = add(near, own_ref[date, a, 0], own_ref[date, a, 1], x_re, x_im)
                    far = add(far, h_re, h_im, x_re, x_im)
                    far = add(far, cov_a[date + half, a, 0], cov_a[date + half, a, 1], w_re, w_im)
                    return near, far

                zero = jnp.zeros((half, LANES), jnp.float32)
                near, far = lax.fori_loop(0, half, turn, ((zero, zero), (zero, zero)), unroll=8)
                u_re = jnp.concatenate([near[0] + low_ref[0], far[0]], axis=0) * inv
                u_im = jnp.concatenate([near[1] + low_ref[1], far[1]], axis=0) * inv
                length = 1.0 / jnp.sqrt(u_re * u_re + u_im * u_im + PROJ_LOAD)
                vec_re = u_re * length
                vec_im = u_im * length
            out_ref[a, 0] = vec_re
            out_ref[a, 1] = vec_im
            return carry

        lax.fori_loop(0, wins, window, 0)


def call_windows(groups, mask, win_cols, own=None):
    count, lines = groups[0].shape[1:3]
    dates = count * len(groups)
    wins = lines // 4 - 3
    steps = 2 * (win_cols // LANES) + 1
    pitch = -(-lines // 8) * 8
    column = np.arange(STEP)[:, None]
    window = np.arange(LANES)[None, :]
    band = lambda shift: ((column + shift >= 4 * window) & (column + shift < 4 * window + 16)).astype(np.float32)
    zero = np.zeros((STEP, LANES), np.float32)
    bands = np.stack(
        [
            np.concatenate([band(2 * STEP), band(0)], axis=1),
            np.concatenate([zero, band(STEP)], axis=1),
        ]
    ).astype(jnp.bfloat16)
    f32 = jnp.float32
    place = lambda t: jnp.maximum((t + 1) // 2 - 1, 0)
    cov_spec = pl.BlockSpec((count, wins, 2, count, LANES), lambda t: (0, 0, 0, 0, place(t)))
    in_specs = [pl.BlockSpec((2, count, lines, STEP), lambda t: (0, 0, 0, t)) for _ in groups]
    in_specs.append(pl.BlockSpec((lines, STEP), lambda t: (0, t)))
    in_specs.append(pl.BlockSpec((1, STEP, 2 * LANES), lambda t: (t % 2, 0, 0)))
    operands = list(groups) + [mask, bands]
    scratch = [
        pltpu.VMEM((2, 2 * dates * pitch, LANES), f32),
        pltpu.VMEM((2, lines, count, LANES), f32),
        pltpu.VMEM((2, lines, count, LANES), f32),
        pltpu.VMEM((2, lines, dates, LANES), f32),
        pltpu.VMEM((2, lines, dates, LANES), f32),
        pltpu.VMEM((2, lines, LANES), f32),
        pltpu.VMEM((2, 2, wins, 2, count, STEP), jnp.bfloat16),
        pltpu.VMEM((dates, wins, 2, count, LANES), f32),
    ]
    if own is None:
        kernel = own_kernel
        out_spec = cov_spec
        out_shape = (count, wins, 2, count, win_cols)
    else:
        kernel = link_kernel
        in_specs.append(cov_spec)
        operands.append(own)
        out_spec = pl.BlockSpec((wins, 2, dates, LANES), lambda t: (0, 0, 0, place(t)))
        out_shape = (wins, 2, dates, win_cols)
        scratch += [
            pltpu.VMEM((dates, wins, 2, count, LANES), f32),
            pltpu.VMEM((2, dates, LANES), f32),
            pltpu.VMEM((2, count, LANES), f32),
            pltpu.VMEM((dates, LANES), f32),
        ]
    return pl.pallas_call(
        kernel,
        grid=(steps,),
        in_specs=in_specs,
        out_specs=out_spec,
        out_shape=jax.ShapeDtypeStruct(out_shape, f32),
        scratch_shapes=scratch,
        cost_estimate=pl.CostEstimate(flops=steps * 10**8, bytes_accessed=10**6, transcendentals=0),
        compiler_params=pltpu.CompilerParams(vmem_limit_bytes=56 * 2**20),
    )(*operands)


def on_device(stack, range_filter, scatter_mask):
    parts = lax.axis_size("dr")
    own = lax.axis_index("dr")
    dates_here, lines, samples = stack.shape[1:]
    tile = samples // parts
    width = tile + 2 * HALO
    win_cols = tile // 4
    padded_width = STEP * (2 * (win_cols // LANES) + 1)

    def cut(array, number):
        wide = jnp.pad(array, ((0, 0),) * (array.ndim - 1) + ((HALO, HALO),))
        return lax.dynamic_slice_in_dim(wide, number * tile, width, array.ndim - 1)

    def edges(array):
        dim = array.ndim - 2
        count = lax.axis_size("az")
        head = lax.slice_in_dim(array, 0, HALO, axis=dim)
        tail = lax.slice_in_dim(array, lines - HALO, lines, axis=dim)
        before = lax.ppermute(tail, "az", [(i, i + 1) for i in range(count - 1)])
        after = lax.ppermute(head, "az", [(i + 1, i) for i in range(count - 1)])
        return jnp.concatenate([before, array, after], axis=dim)

    def spare(array):
        return jnp.pad(array, ((0, 0),) * (array.ndim - 1) + ((0, padded_width - width),))

    mask = spare(edges(cut(scatter_mask, own).astype(jnp.bfloat16))).astype(jnp.float32)
    pieces = [[] for _ in range(parts)]
    for chunk in range(CHUNKS):
        filtered = filter_lines(stack, range_filter, chunk, CHUNKS)
        sent = [cut(filtered, lax.rem(own + shift, parts)) for shift in range(1, parts)]
        stack, sent = lax.optimization_barrier((stack, sent))
        pieces[0].append(cut(filtered, own))
        for shift in range(1, parts):
            pieces[shift].append(lax.ppermute(sent[shift - 1], "dr", [(i, (i + shift) % parts) for i in range(parts)]))
    near = sum(pieces[: parts // 2], [])
    far = sum(pieces[parts // 2 :], [])
    near = spare(edges(jnp.concatenate(near, axis=1)))
    own_sums = call_windows([near], mask, win_cols)
    own_sums, far = lax.optimization_barrier((own_sums, far))
    far = spare(edges(jnp.concatenate(far, axis=1)))
    linked = call_windows([near, far], mask, win_cols, own_sums)
    wins = linked.shape[0]
    linked = jnp.transpose(linked, (1, 2, 0, 3)).reshape(2, parts, dates_here, wins, win_cols)
    ordered = [
        lax.dynamic_index_in_dim(linked, lax.rem(own - t + parts, parts), 1, keepdims=False) for t in range(parts)
    ]
    return jnp.concatenate(ordered, axis=1)


def solution(mesh):
    in_specs = (P(None, "dr", "az", None), P("dr", None), P("az", None))
    out_specs = P(None, None, "az", "dr")
    return jax.shard_map(on_device, mesh=mesh, in_specs=in_specs, out_specs=out_specs, check_vma=False)
```

```python
import functools
import math

import jax
import jax.numpy as jnp
import numpy as np
from jax import lax
from jax.experimental import pallas as pl
from jax.experimental.pallas import tpu as pltpu
from jax.sharding import PartitionSpec as P

ITERS = 4
BETA_LOAD = 1.0
PROJ_LOAD = 1.0
LANES = 128
STEP = 256
HALO = 6


def times_const(value, c, s):
    re, im = value
    if abs(s) < 1e-12:
        return (re, im) if c > 0 else (-re, -im)
    if abs(c) < 1e-12:
        return (-im, re) if s > 0 else (im, -re)
    if abs(abs(c) - abs(s)) < 1e-12:
        h = abs(c)
        sc, ss = (1.0 if c > 0 else -1.0), (1.0 if s > 0 else -1.0)
        a = re if sc == 1.0 else -re
        b = im if sc == 1.0 else -im
        return (h * (a - im if ss == 1.0 else a + im), h * (b + re if ss == 1.0 else b - re))
    return (re * c - im * s, re * s + im * c)


def vector_fft(values, sign):
    count = len(values)
    if count == 1:
        return values
    even = vector_fft(values[0::2], sign)
    odd = vector_fft(values[1::2], sign)
    out = [None] * count
    for k in range(count // 2):
        angle = sign * 2.0 * math.pi * k / count
        tr, ti = times_const(odd[k], math.cos(angle), math.sin(angle))
        er, ei = even[k]
        out[k] = (er + tr, ei + ti)
        out[k + count // 2] = (er - tr, ei - ti)
    return out


def filter_kernel(outer, x_ref, gain_ref, twr_ref, twi_ref, tab_ref, out_ref, field, work):
    lines = x_ref.shape[2]
    samples = outer * LANES
    field[...] = x_ref[:, 0].astype(jnp.float32)
    groups = lines // 8

    def forward(g, carry):
        rows = pl.ds(pl.multiple_of(g * 8, 8), 8)
        vals = [
            (field[0, rows, o * LANES : (o + 1) * LANES], field[1, rows, o * LANES : (o + 1) * LANES])
            for o in range(outer)
        ]
        vals = vector_fft(vals, -1.0)
        for o in range(outer):
            re, im = vals[o]
            c, s = twr_ref[o : o + 1, :], twi_ref[o : o + 1, :]
            work[o, rows, 0:LANES] = re * c - im * s
            work[o, rows, LANES:STEP] = re * s + im * c
        return carry

    lax.fori_loop(0, groups, forward, 0)

    def apply(values, way):
        high = values.astype(jnp.bfloat16)
        low = (values - high.astype(jnp.float32)).astype(jnp.bfloat16)
        dot = functools.partial(jnp.dot, preferred_element_type=jnp.float32)
        return dot(high, tab_ref[way]) + (dot(low, tab_ref[way]) + dot(high, tab_ref[way + 2]))

    part = 8

    def middle(q, carry):
        span = pl.ds(q * part, part)
        values = work[span].reshape(part * lines, STEP)
        spec = apply(values, 0).reshape(part, lines, STEP)
        gains = gain_ref[0, pl.ds(pl.multiple_of(q * part, part), part), :]
        both = jnp.concatenate([gains, gains], axis=1)[:, None, :]
        spec = (spec * both).reshape(part * lines, STEP)
        work[span] = apply(spec, 1).reshape(part, lines, STEP)
        return carry

    lax.fori_loop(0, outer // part, middle, 0)

    def backward(g, carry):
        rows = pl.ds(pl.multiple_of(g * 8, 8), 8)
        vals = []
        for o in range(outer):
            re, im = work[o, rows, 0:LANES], work[o, rows, LANES:STEP]
            c, s = twr_ref[o : o + 1, :], twi_ref[o : o + 1, :]
            vals.append((re * c + im * s, im * c - re * s))
        vals = vector_fft(vals, 1.0)
        for o in range(outer):
            field[0, rows, o * LANES : (o + 1) * LANES] = vals[o][0] * (1.0 / samples)
            field[1, rows, o * LANES : (o + 1) * LANES] = vals[o][1] * (1.0 / samples)
        return carry

    lax.fori_loop(0, groups, backward, 0)
    out_ref[:, 0] = field[...].astype(jnp.bfloat16)


def split_table(table):
    high = table.astype(jnp.bfloat16)
    return high, (table - np.asarray(high).astype(np.float32)).astype(jnp.bfloat16)


def filter_lines(stack, gains, skip, here):
    dates, lines, samples = stack.shape[1:]
    outer = samples // LANES
    n = np.arange(LANES)
    angle = -2.0 * np.pi * (n[:, None] * n[None, :] % LANES) / LANES
    c, s = np.cos(angle), np.sin(angle)
    fwd = np.block([[c, s], [-s, c]]).astype(np.float32)
    bwd = np.block([[c, -s], [s, c]]).astype(np.float32)
    twist = -2.0 * np.pi * (np.arange(outer)[:, None] * n[None, :]) / samples
    fh, fl = split_table(fwd)
    bh, bl = split_table(bwd)
    gain_table = jnp.transpose(gains.reshape(dates, LANES, outer), (0, 2, 1))
    whole = lambda *shape: pl.BlockSpec(shape, lambda d: (0,) * len(shape))
    return pl.pallas_call(
        functools.partial(filter_kernel, outer),
        grid=(here,),
        in_specs=[
            pl.BlockSpec((2, 1, lines, samples), lambda d: (0, d + skip, 0, 0)),
            pl.BlockSpec((1, outer, LANES), lambda d: (d + skip, 0, 0)),
            whole(outer, LANES),
            whole(outer, LANES),
            whole(4, STEP, STEP),
        ],
        out_specs=pl.BlockSpec((2, 1, lines, samples), lambda d: (0, d, 0, 0)),
        out_shape=jax.ShapeDtypeStruct((2, here, lines, samples), jnp.bfloat16),
        cost_estimate=pl.CostEstimate(flops=here * 10**8, bytes_accessed=10**6, transcendentals=0),
        scratch_shapes=[
            pltpu.VMEM((2, lines, samples), jnp.float32),
            pltpu.VMEM((outer, lines, STEP), jnp.float32),
        ],
        compiler_params=pltpu.CompilerParams(vmem_limit_bytes=40 * 2**20),
    )(
        stack,
        gain_table,
        np.cos(twist).astype(np.float32),
        np.sin(twist).astype(np.float32),
        np.stack([fh, bh, fl, bl]),
    )


def load_planes(width, groups, m_ref, flat, pr, pi, mr, mi, m_half):
    count = groups[0][-1].shape[1]
    lines = m_ref.shape[0]
    dates = count * len(groups)
    pitch = flat.shape[1] // (2 * dates)
    column = lax.broadcasted_iota(jnp.int32, (1, STEP), 1) + pl.program_id(0) * STEP
    inside = column < width

    def put(ref, part, p, place):
        rows = jnp.where(inside, ref[part, p].astype(jnp.float32), 0.0)
        for h in range(2):
            flat[h, place : place + rows.shape[0], :] = rows[:, h * LANES : (h + 1) * LANES]

    for part in range(2):
        for k, (*middle, before, after) in enumerate(groups):
            place = (part * dates + k * count) * pitch
            for p in range(count):
                put(before, part, p, place + p * pitch)
                put(after, part, p, place + p * pitch + lines - HALO)
            for ref in middle:
                for p in range(ref.shape[1]):
                    put(ref, part, p, place + HALO)
                    place += pitch
    for h in range(2):
        m_half[h] = m_ref[:, h * LANES : (h + 1) * LANES]

    def spread(line, carry):
        for h in range(2):
            weight = m_half[h, pl.ds(line, 1), :]
            re = flat[h, pl.ds(line, dates, stride=pitch), :]
            im = flat[h, pl.ds(line + dates * pitch, dates, stride=pitch), :]
            pr[h, line] = re[dates - count :]
            pi[h, line] = im[dates - count :]
            mr[h, line] = re * weight
            mi[h, line] = im * weight
        return carry

    lax.fori_loop(0, lines, spread, 0)


def window_sums(halves, dates, odd, band_ref, pr, pi, mr, mi, wide, cov_a, cov_b):
    count = pr.shape[2]
    blocks = pr.shape[1] // 4
    wins = blocks - 3

    def sums(slot, spot, date):
        for h in range(halves):
            lanes = slice(h * LANES, (h + 1) * LANES)
            last = None
            pairs = []
            for r in range(blocks):
                re = im = None
                for j in range(4):
                    line = 4 * r + j
                    ar = mr[h, line, pl.ds(date, 1), :]
                    ai = mi[h, line, pl.ds(date, 1), :]
                    br = pr[h, line]
                    bi = pi[h, line]
                    t_re = ar * br + ai * bi
                    t_im = ai * br - ar * bi
                    re = t_re if re is None else re + t_re
                    im = t_im if im is None else im + t_im
                if last is not None:
                    pairs.append((last[0] + re, last[1] + im))
                last = (re, im)
                a = r - 3
                if a >= 0:
                    wide[slot, spot, a, 0, :, lanes] = (pairs[a][0] + pairs[a + 2][0]).astype(jnp.bfloat16)
                    wide[slot, spot, a, 1, :, lanes] = (pairs[a][1] + pairs[a + 2][1]).astype(jnp.bfloat16)

    def gather(duo):
        rows = wide[duo % 2].reshape(2 * wins * 2 * count, STEP)
        total = jnp.dot(rows, band_ref[0], preferred_element_type=jnp.float32)
        total = total.reshape(2, wins, 2, count, 2 * LANES)
        span = pl.ds(2 * duo, 2)
        old = cov_b[span]
        cov_a[span] = old + total[..., 0:LANES]
        cov_b[span] = jnp.where(odd, old, 0.0) + total[..., LANES : 2 * LANES]

    def both(duo):
        for spot in range(2):
            sums(duo % 2, spot, 2 * duo + spot)

    both(0)

    def body(duo, carry):
        gather(duo - 1)
        both(duo)
        return carry

    lax.fori_loop(1, dates // 2, body, 0)
    gather(dates // 2 - 1)


def all_sums(dates, *refs):
    step = pl.program_id(0)
    last = step == pl.num_programs(0) - 1
    odd = step % 2 == 1
    pl.when(last)(lambda: window_sums(1, dates, odd, *refs))
    pl.when(jnp.logical_not(last))(lambda: window_sums(2, dates, odd, *refs))


def own_kernel(width, sizes, *refs):
    group = refs[: sizes[0]]
    m_ref, band_ref, cov_ref, flat, pr, pi, mr, mi, m_half, wide, cov_b = refs[sizes[0] :]
    load_planes(width, [group], m_ref, flat, pr, pi, mr, mi, m_half)
    all_sums(group[-1].shape[1], band_ref, pr, pi, mr, mi, wide, cov_ref, cov_b)


def link_kernel(width, sizes, *refs):
    groups = [refs[: sizes[0]], refs[sizes[0] : sum(sizes)]]
    (m_ref, band_ref, own_ref, out_ref, flat, pr, pi, mr, mi, m_half, wide, cov_b, cov_a, y_ref, low_ref, diag) = refs[
        sum(sizes) :
    ]
    step = pl.program_id(0)
    half = groups[0][-1].shape[1]
    dates = 2 * half
    wins = m_ref.shape[0] // 4 - 3
    load_planes(width, groups, m_ref, flat, pr, pi, mr, mi, m_half)
    all_sums(dates, band_ref, pr, pi, mr, mi, wide, cov_a, cov_b)

    @pl.when((step % 2 == 0) & (step > 0))
    def _():
        def window(a, carry):
            def pick(date, c):
                diag[pl.ds(date, 1), :] = own_ref[date, a, 0, pl.ds(date, 1), :]
                diag[pl.ds(date + half, 1), :] = cov_a[date + half, a, 0, pl.ds(date, 1), :]
                return c

            lax.fori_loop(0, half, pick, 0)
            inv = 1.0 / jnp.sqrt(diag[...] + BETA_LOAD)
            vec_re = jnp.ones_like(inv)
            vec_im = jnp.zeros_like(inv)

            def add(acc, c_re, c_im, x_re, x_im):
                return (acc[0] + (c_re * x_re + c_im * x_im), acc[1] + (c_re * x_im - c_im * x_re))

            for repeat in range(ITERS):
                y_ref[0] = vec_re * inv
                y_ref[1] = vec_im * inv
                far_re, far_im = y_ref[0, half:dates], y_ref[1, half:dates]

                def turn(date, acc):
                    near, far = acc
                    x_re, x_im = y_ref[0, pl.ds(date, 1), :], y_ref[1, pl.ds(date, 1), :]
                    w_re, w_im = y_ref[0, pl.ds(date + half, 1), :], y_ref[1, pl.ds(date + half, 1), :]
                    h_re, h_im = cov_a[date, a, 0], cov_a[date, a, 1]
                    low_ref[0, pl.ds(date, 1), :] = jnp.sum(h_re * far_re - h_im * far_im, axis=0, keepdims=True)
                    low_ref[1, pl.ds(date, 1), :] = jnp.sum(h_re * far_im + h_im * far_re, axis=0, keepdims=True)
                    near = add(near, own_ref[date, a, 0], own_ref[date, a, 1], x_re, x_im)
                    far = add(far, h_re, h_im, x_re, x_im)
                    far = add(far, cov_a[date + half, a, 0], cov_a[date + half, a, 1], w_re, w_im)
                    return near, far

                zero = jnp.zeros((half, LANES), jnp.float32)
                near, far = lax.fori_loop(0, half, turn, ((zero, zero), (zero, zero)), unroll=8)
                u_re = jnp.concatenate([near[0] + low_ref[0], far[0]], axis=0) * inv
                u_im = jnp.concatenate([near[1] + low_ref[1], far[1]], axis=0) * inv
                length = 1.0 / jnp.sqrt(u_re * u_re + u_im * u_im + PROJ_LOAD)
                vec_re = u_re * length
                vec_im = u_im * length
            out_ref[a, 0] = vec_re
            out_ref[a, 1] = vec_im
            return carry

        lax.fori_loop(0, wins, window, 0)


def call_windows(groups, mask, win_cols, own=None):
    count = groups[0][-1].shape[1]
    lines = mask.shape[0]
    width = groups[0][0].shape[3]
    sizes = [len(group) for group in groups]
    dates = count * len(groups)
    wins = lines // 4 - 3
    steps = 2 * (win_cols // LANES) + 1
    pitch = -(-lines // 8) * 8
    column = np.arange(STEP)[:, None]
    window = np.arange(LANES)[None, :]
    band = lambda shift: ((column + shift >= 4 * window) & (column + shift < 4 * window + 16)).astype(np.float32)
    zero = np.zeros((STEP, LANES), np.float32)
    bands = np.stack(
        [
            np.concatenate([band(2 * STEP), band(0)], axis=1),
            np.concatenate([zero, band(STEP)], axis=1),
        ]
    ).astype(jnp.bfloat16)
    f32 = jnp.float32
    place = lambda t: jnp.maximum((t + 1) // 2 - 1, 0)
    cov_spec = pl.BlockSpec((count, wins, 2, count, LANES), lambda t: (0, 0, 0, 0, place(t)))
    operands = [array for group in groups for array in group]
    in_specs = [pl.BlockSpec(array.shape[:3] + (STEP,), lambda t: (0, 0, 0, t)) for array in operands]
    in_specs.append(pl.BlockSpec((lines, STEP), lambda t: (0, t)))
    in_specs.append(pl.BlockSpec((1, STEP, 2 * LANES), lambda t: (t % 2, 0, 0)))
    operands += [mask, bands]
    scratch = [
        pltpu.VMEM((2, 2 * dates * pitch, LANES), f32),
        pltpu.VMEM((2, lines, count, LANES), f32),
        pltpu.VMEM((2, lines, count, LANES), f32),
        pltpu.VMEM((2, lines, dates, LANES), f32),
        pltpu.VMEM((2, lines, dates, LANES), f32),
        pltpu.VMEM((2, lines, LANES), f32),
        pltpu.VMEM((2, 2, wins, 2, count, STEP), jnp.bfloat16),
        pltpu.VMEM((dates, wins, 2, count, LANES), f32),
    ]
    if own is None:
        kernel = own_kernel
        out_spec = cov_spec
        out_shape = (count, wins, 2, count, win_cols)
    else:
        kernel = link_kernel
        in_specs.append(cov_spec)
        operands.append(own)
        out_spec = pl.BlockSpec((wins, 2, dates, LANES), lambda t: (0, 0, 0, place(t)))
        out_shape = (wins, 2, dates, win_cols)
        scratch += [
            pltpu.VMEM((dates, wins, 2, count, LANES), f32),
            pltpu.VMEM((2, dates, LANES), f32),
            pltpu.VMEM((2, count, LANES), f32),
            pltpu.VMEM((dates, LANES), f32),
        ]
    return pl.pallas_call(
        functools.partial(kernel, width, sizes),
        grid=(steps,),
        in_specs=in_specs,
        out_specs=out_spec,
        out_shape=jax.ShapeDtypeStruct(out_shape, f32),
        scratch_shapes=scratch,
        cost_estimate=pl.CostEstimate(flops=steps * 10**8, bytes_accessed=10**6, transcendentals=0),
        compiler_params=pltpu.CompilerParams(vmem_limit_bytes=56 * 2**20),
    )(*operands)


def on_device(stack, range_filter, scatter_mask):
    parts = lax.axis_size("dr")
    own = lax.axis_index("dr")
    dates_here, lines, samples = stack.shape[1:]
    tile = samples // parts
    width = tile + 2 * HALO
    win_cols = tile // 4
    padded_width = STEP * (2 * (win_cols // LANES) + 1)

    def cut(array, number):
        wide = jnp.pad(array, ((0, 0),) * (array.ndim - 1) + ((HALO, HALO),))
        return lax.dynamic_slice_in_dim(wide, number * tile, width, array.ndim - 1)

    def edges(arrays):
        count = lax.axis_size("az")
        dim = arrays[0].ndim - 2
        join = lambda start: jnp.concatenate([lax.slice_in_dim(a, start, start + HALO, axis=dim) for a in arrays], axis=dim - 1)
        before = lax.ppermute(join(lines - HALO), "az", [(i, i + 1) for i in range(count - 1)])
        after = lax.ppermute(join(0), "az", [(i + 1, i) for i in range(count - 1)])
        return [before, after]

    mask = cut(scatter_mask, own).astype(jnp.bfloat16)
    above, below = edges([mask[None]])
    mask = jnp.concatenate([above[0], mask, below[0]], axis=0)
    mask = jnp.pad(mask, ((0, 0), (0, padded_width - width))).astype(jnp.float32)
    first = max(1, dates_here // 4)
    pieces = [[] for _ in range(parts)]
    for skip, here in ((0, first), (first, dates_here - first)):
        filtered = filter_lines(stack, range_filter, skip, here)
        sent = [cut(filtered, lax.rem(own + shift, parts)) for shift in range(1, parts)]
        stack, sent = lax.optimization_barrier((stack, sent))
        pieces[0].append(cut(filtered, own))
        for shift in range(1, parts):
            pieces[shift].append(lax.ppermute(sent[shift - 1], "dr", [(i, (i + shift) % parts) for i in range(parts)]))
    near = sum(pieces[: parts // 2], [])
    far = sum(pieces[parts // 2 :], [])
    near, far[0] = lax.optimization_barrier((near, far[0]))
    near = near + edges(near)
    own_sums = call_windows([near], mask, win_cols)
    own_sums, far = lax.optimization_barrier((own_sums, far))
    linked = call_windows([near, far + edges(far)], mask, win_cols, own_sums)
    wins = linked.shape[0]
    linked = jnp.transpose(linked, (1, 2, 0, 3)).reshape(2, parts, dates_here, wins, win_cols)
    ordered = [
        lax.dynamic_index_in_dim(linked, lax.rem(own - t + parts, parts), 1, keepdims=False) for t in range(parts)
    ]
    return jnp.concatenate(ordered, axis=1)


def solution(mesh):
    in_specs = (P(None, "dr", "az", None), P("dr", None), P("az", None))
    out_specs = P(None, None, "az", "dr")
    return jax.shard_map(on_device, mesh=mesh, in_specs=in_specs, out_specs=out_specs, check_vma=False)
```
